128 devices in a mesh: mem: 8 (over z, core), blk: 16 (over x, y).
Axes of the slice: x: 4, y: 4, z: 4, core: 2. Of those that a mesh axis runs over, the one named last changes fastest.
Arguments:
- members: bfloat16 [128, 64, 128, 256], P(('mem', 'blk')), may hold values from -6 to 6
- obs_cell: int32 [64, 128, 128], P('mem', 'blk'), may hold values from 0 to 255
- obs_value: float32 [64, 128, 128], P('mem', 'blk'), may hold values from -8 to 8
- obs_rinv: float32 [64, 128, 128], P('mem', 'blk'), may hold values from 0.25 to 4
- obs_count: int32 [64, 128], P('mem', 'blk'), may hold values from 1 to 128
- loc_pattern: int32 [64, 128, 9], P('mem', 'blk'), may hold values 0 or 1
Outputs:
- analysis: bfloat16 [128, 64, 128, 256], P(('mem', 'blk'))
The draws below stay inside these ranges and needn't reach their ends.
All inputs are finite; a program needn't handle non-finite values. No bound on the sum of `loc_pattern` on one device may be relied on, other than what follows from the above.
Results may differ from the reference program's by a relative error of at most 0.013.
Values may be sent and summed in bfloat16 or wider, within the bound.
No kernel may reach another device: no remote copies, remote signals or barrier semaphores. Data moves between devices by JAX's collectives and lax.ppermute only.
A program may use at most 128 MiB of HBM per device.

```python
import math
import jax
import jax.numpy as jnp
from jax import lax

K = 128
BC = 256
OBS = 128
NS_STEPS = 5
NLAT = 64
NLON = 128


def plant(values, own_key, low, largest):
    index_at = [jax.random.randint(jax.random.fold_in(own_key, axis), (), 0, length) for axis, length in enumerate(values.shape)]
    longest = values.shape.index(max(values.shape))
    neighbour = index_at[:longest] + [(index_at[longest] + 1) % values.shape[longest]] + index_at[longest + 1:]
    return values.at[tuple(index_at)].set(low).at[tuple(neighbour)].set(largest)


def block_levels(rng, shape, shards, smallest, top_value):
    factor_of = 1.0
    for dim, shards_of in shards:
        draws = jax.random.uniform(jax.random.fold_in(jax.random.fold_in(rng, 6), dim), (shards_of,), jnp.float32, smallest / len(shards), top_value / len(shards))
        factor_of = factor_of * jnp.repeat(jnp.exp(draws), shape[dim] // shards_of).reshape((-1,) + (1,) * (len(shape) - 1 - dim))
    return factor_of


def noise(key, shape, scale, limit, cuts=(), kind=jnp.bfloat16):
    entries = scale * jax.random.normal(key, shape, jnp.float32)
    if cuts:
        entries = entries * block_levels(key, shape, cuts, -0.22, 0.18)
    return jnp.clip(entries, -limit, limit).astype(kind)


def setup_inputs(seed: int = 0) -> dict:
    seeds = jax.random.split(jax.random.key(seed), 7)
    members = noise(seeds[0], (K, NLAT, NLON, BC), 1.0, 6.0, ((0, 128),))
    obs_cell = plant(jax.random.randint(seeds[1], (NLAT, NLON, OBS), 0, BC), jax.random.fold_in(seeds[1], 1), 0, BC - 1).astype(jnp.int32)
    obs_value = noise(seeds[2], (NLAT, NLON, OBS), 1.5, 8.0, ((0, 8), (1, 16)), jnp.float32)
    obs_rinv = jnp.clip(jnp.exp(math.log(4.0) - 2.7725887 * jax.random.uniform(seeds[3], (NLAT, NLON, OBS), jnp.float32) ** block_levels(seeds[3], (NLAT, NLON, OBS), ((0, 8), (1, 16)), -0.2, 0.2)), 0.25, 4.0)
    obs_count = plant(jax.random.randint(seeds[4], (NLAT, NLON), 1, OBS + 1), jax.random.fold_in(seeds[4], 1), 1, OBS).astype(jnp.int32)
    loc_pattern = plant((jax.random.randint(seeds[5], (NLAT, NLON, 9), 0, 4) < 3).astype(jnp.int32), jax.random.fold_in(seeds[5], 1), 0, 1)
    return dict(members=members, obs_cell=obs_cell, obs_value=obs_value, obs_rinv=obs_rinv, obs_count=obs_count, loc_pattern=loc_pattern)


TAPER_WEIGHTS = (0.3, 0.6, 0.3, 0.6, 1.0, 0.6, 0.3, 0.6, 0.3)
INFLATION = 1.1

def obs_payload(state, obs_cell, obs_value, obs_rinv, obs_count):
    positions = jnp.broadcast_to(obs_cell[None], (state.shape[0],) + obs_cell.shape)
    obs_ens = jnp.take_along_axis(state, positions, axis=3).astype(jnp.float32)
    obs_mean = lax.optimization_barrier(jnp.mean(obs_ens, axis=0))
    spread_obs = jnp.moveaxis(obs_ens - obs_mean[None], 0, 2)
    departure = obs_value - obs_mean
    live = (lax.broadcasted_iota(jnp.int32, obs_value.shape, 2) < obs_count[:, :, None]).astype(jnp.float32)
    obs_weight = obs_rinv * live
    return jnp.concatenate([spread_obs, departure[:, :, None], obs_weight[:, :, None]], axis=2)

def analyse_row(three_rows, pattern_row, state_row):
    highest = lax.Precision.HIGHEST
    lon_cols = state_row.shape[0]
    members = state_row.shape[1]
    obs_slots = three_rows.shape[3]
    neighbours = jnp.stack([three_rows[:, offset:offset + lon_cols] for offset in range(3)], axis=1)
    neighbours = neighbours.reshape(9, lon_cols, members + 2, obs_slots)
    neighbours = jnp.transpose(neighbours, (1, 2, 0, 3)).reshape(lon_cols, members + 2, 9 * obs_slots)
    spread_obs = neighbours[:, :members]
    departure = neighbours[:, members]
    taper_row = jnp.asarray(TAPER_WEIGHTS, jnp.float32)[None, :] * pattern_row.astype(jnp.float32)
    obs_weight = neighbours[:, members + 1] * jnp.repeat(taper_row, obs_slots, axis=1)
    scaled = spread_obs * obs_weight[:, None, :]
    identity = jnp.eye(members, dtype=jnp.float32)
    info_matrix = (members - 1) / INFLATION * identity + jnp.einsum('bkp,blp->bkl', scaled, spread_obs, precision=highest)
    scale_norm = jnp.sqrt(lax.optimization_barrier(jnp.sum(info_matrix * info_matrix, axis=(1, 2))))
    iter_p = info_matrix / scale_norm[:, None, None]
    iter_q = jnp.broadcast_to(identity, iter_p.shape)
    for sweep in range(NS_STEPS):
        factor = 1.5 * identity - 0.5 * jnp.einsum('bij,bjk->bik', iter_q, iter_p, precision=highest)
        iter_p, iter_q = (jnp.einsum('bij,bjk->bik', iter_p, factor, precision=highest), jnp.einsum('bij,bjk->bik', factor, iter_q, precision=highest))
    covariance = jnp.einsum('bij,bjk->bik', iter_q, iter_q, precision=highest) / scale_norm[:, None, None]
    gain_in = jnp.einsum('bkp,bp->bk', scaled, departure, precision=highest)
    mean_weights = jnp.einsum('bkl,bl->bk', covariance, gain_in, precision=highest)
    transform = jnp.sqrt((members - 1) / scale_norm)[:, None, None] * iter_q + mean_weights[:, :, None]
    background = state_row.astype(jnp.float32)
    ens_mean = lax.optimization_barrier(jnp.mean(background, axis=1, keepdims=True))
    perturb = background - ens_mean
    result = ens_mean + jnp.einsum('bik,bic->bkc', transform, perturb, precision=highest)
    return result.astype(jnp.bfloat16)

def reference(members, obs_cell, obs_value, obs_rinv, obs_count, loc_pattern):
    payload = obs_payload(members, obs_cell, obs_value, obs_rinv, obs_count)
    padded = jnp.pad(payload, ((1, 1), (0, 0), (0, 0), (0, 0)))
    padded = jnp.concatenate([padded[:, -1:], padded, padded[:, :1]], axis=1)
    state_rows = jnp.moveaxis(members, 0, 2)

    def one_row(inputs):
        row_index, pattern_row, state_row = inputs
        three_rows = lax.dynamic_slice_in_dim(padded, row_index, 3, 0)
        return analyse_row(three_rows, pattern_row, state_row)
    rows = lax.map(one_row, (jnp.arange(NLAT, dtype=jnp.int32), loc_pattern, state_rows))
    return jnp.moveaxis(rows, 2, 0)
```

```python
import jax
import jax.numpy as jnp
from jax import lax
from jax.experimental import pallas as pl
from jax.experimental.pallas import tpu as pltpu
from jax.sharding import PartitionSpec as P

NS_STEPS = 5
TAPER_WEIGHTS = (0.3, 0.6, 0.3, 0.6, 1.0, 0.6, 0.3, 0.6, 0.3)
INFLATION = 1.1
F32 = jnp.float32
BF16 = jnp.bfloat16
PAD = 16
LANES = 128
AXES = ("mem", "blk")
VMEM_LIMIT = 48 * 1024 * 1024


def select_kernel(x_ref, cell_ref, value_ref, root_ref, xt_ref, gh_ref, wide):
    members, group, cells = x_ref.shape
    slots = cell_ref.shape[1]
    for k in range(0, members, 16):
        part = x_ref[k : k + 16].astype(F32).reshape(16 * group, cells)
        for h in range(cells // LANES):
            wide[h, k * group : (k + 16) * group, :] = part[:, h * LANES : (h + 1) * LANES]
    ids = lax.broadcasted_iota(jnp.int32, (cells, slots), 0)
    pad_row = lax.broadcasted_iota(jnp.int32, (PAD, slots), 0)

    def block(b, carry):
        state = jnp.concatenate(
            [
                wide[h, pl.ds(b, members, stride=group), :].astype(BF16)
                for h in range(cells // LANES)
            ],
            axis=1,
        )
        xt_ref[b] = state
        selector = (ids == cell_ref[pl.ds(b, 1), :]).astype(BF16)
        obs = jnp.dot(state, selector, preferred_element_type=F32)
        mean = jnp.sum(obs, axis=0, keepdims=True) * (1.0 / members)
        root = root_ref[pl.ds(b, 1), :]
        rooted = ((obs - mean) * root).astype(BF16)
        depart = (value_ref[pl.ds(b, 1), :] - mean) * root
        high = depart.astype(BF16).astype(F32)
        extra = jnp.where(pad_row == 0, high, jnp.where(pad_row == 1, depart - high, 0.0))
        left = jnp.concatenate([rooted, extra.astype(BF16)], axis=0)
        gram = lax.dot_general(
            left, rooted, (((1,), (1,)), ((), ())), preferred_element_type=F32
        )
        gain = gram[members : members + 1] + gram[members + 1 : members + 2]
        gain_high = gain.astype(BF16).astype(F32)
        tail = jnp.where(pad_row == 0, gain_high, jnp.where(pad_row == 1, gain - gain_high, 0.0))
        gh_ref[b, :members] = gram[:members].astype(BF16)
        gh_ref[b, members:] = tail.astype(BF16)
        return carry

    lax.fori_loop(0, group, block, 0, unroll=2)


def select(state, cell, value, root):
    members, blocks, cells = state.shape
    slots = cell.shape[1]
    group = 16
    row = pl.BlockSpec((group, slots), lambda i: (i, 0))
    return pl.pallas_call(
        select_kernel,
        grid=(blocks // group,),
        in_specs=[pl.BlockSpec((members, group, cells), lambda i: (0, i, 0)), row, row, row],
        out_specs=[
            pl.BlockSpec((group, members, cells), lambda i: (i, 0, 0)),
            pl.BlockSpec((group, members + PAD, members), lambda i: (i, 0, 0)),
        ],
        out_shape=[
            jax.ShapeDtypeStruct((blocks, members, cells), BF16),
            jax.ShapeDtypeStruct((blocks, members + PAD, members), BF16),
        ],
        scratch_shapes=[pltpu.VMEM((cells // LANES, members * group, LANES), F32)],
        compiler_params=pltpu.CompilerParams(vmem_limit_bytes=VMEM_LIMIT),
        cost_estimate=pl.CostEstimate(
            flops=blocks * 2 * members * slots * (cells + members),
            bytes_accessed=blocks * (4 * members * cells + 2 * (members + PAD) * members),
            transcendentals=0,
        ),
        name="select",
    )(state, cell, value, root)


def analyse_lat(gh, xt, weight, first, pq_f, pq_b, bd, wide, stride, offset):
    cols, members, cells = xt.shape
    c = members
    pairs = cols // 2
    eye = (
        lax.broadcasted_iota(jnp.int32, (members, members), 0)
        == lax.broadcasted_iota(jnp.int32, (members, members), 1)
    )
    ident = eye.astype(F32)
    norms = []
    gains = []
    for j in range(cols):
        acc = None
        for n in range(9):
            term = gh[n // 3, j + n % 3].astype(F32) * weight[(first + j) * 9 + n]
            acc = term if acc is None else acc + term
        info = acc[:members] + (members - 1) / INFLATION * ident
        gains.append(acc[members : members + 1] + acc[members + 1 : members + 2])
        inv = lax.rsqrt(jnp.sum(jnp.sum(info * info, axis=0, keepdims=True), axis=1, keepdims=True))
        norms.append(inv)
        p = info * inv
        third = p * (1.0 / 3.0)
        lanes = slice((j % 2) * c, (j % 2) * c + c)
        pq_f[j // 2, :c, lanes] = p
        pq_b[j // 2, :c, lanes] = p.astype(BF16)
        q = ident - third
        pq_f[j // 2, c:, lanes] = q
        pq_b[j // 2, c:, lanes] = q.astype(BF16)
        bd[j // 2, lanes, lanes] = third.astype(BF16)
    for t in range(pairs):
        p = pq_f[t, :c] - jnp.dot(pq_b[t, :c], bd[t], preferred_element_type=F32)
        pq_f[t, :c] = p
        pq_b[t, :c] = p.astype(BF16)
    for step in range(1, NS_STEPS):
        for t in range(pairs):
            bd[t, :c, :c] = pq_b[t, :c, :c]
            bd[t, c:, c:] = pq_b[t, :c, c:]
        scale = 1.5 ** (2 * step) / 3.0
        for t in range(pairs):
            prod = jnp.dot(pq_b[t, c:], bd[t], preferred_element_type=F32) * scale
            bd[t, :c, :c] = prod[:, :c].astype(BF16)
            bd[t, c:, c:] = prod[:, c:].astype(BF16)
        start = 0 if step < NS_STEPS - 1 else c
        for t in range(pairs):
            new = pq_f[t, start:] - jnp.dot(pq_b[t, start:], bd[t], preferred_element_type=F32)
            pq_f[t, start:] = new
            if start == 0:
                pq_b[t] = new.astype(BF16)
    ones = jnp.full((PAD, members), 1.0 / members, BF16)
    growth = 1.5**NS_STEPS
    for j in range(cols):
        lanes = slice((j % 2) * c, (j % 2) * c + c)
        q = pq_f[j // 2, c:, lanes] * growth
        inv = norms[j]
        column = jnp.sum(q * gains[j], axis=1, keepdims=True)
        weights_row = jnp.sum(q * column, axis=0, keepdims=True) * inv
        transform = (q * jnp.sqrt((members - 1.0) * inv) + weights_row).astype(BF16)
        rest = 1.0 - jnp.sum(transform.astype(F32), axis=1, keepdims=True)
        left = jnp.concatenate([transform, ones], axis=0)
        out = jnp.dot(left, xt[j], preferred_element_type=F32)
        out = out[:members] + rest * out[members : members + 1]
        for h in range(cells // LANES):
            wide[h, pl.ds(offset + j, members, stride=stride), :] = (
                out[:, h * LANES : (h + 1) * LANES]
            )


def analyse(rows, weight, sources, plan, members, cols, cells):
    count = len(rows)
    blocks = count * cols
    c = members

    def kernel(*refs):
        weight_ref = refs[0]
        src = refs[1 : 1 + len(sources)]
        out_ref, gh, xt, pq_f, pq_b, bd, wide, sem = refs[1 + len(sources) :]
        handles = []
        for i in range(count):
            mine = []
            for which, index, kind, place in plan[i]:
                if kind == "x":
                    dst = xt.at[i]
                elif kind == "own":
                    dst = gh.at[i, place, pl.ds(1, cols)]
                else:
                    dst = gh.at[i, place, pl.ds(kind[0], kind[1])]
                handle = pltpu.make_async_copy(src[which].at[index], dst, sem.at[i])
                handle.start()
                mine.append(handle)
            handles.append(mine)
        bd[...] = jnp.zeros_like(bd)
        for i in range(count):
            for handle in handles[i]:
                handle.wait()

        def lat(i, carry):
            first = jnp.where(i == 0, rows[0], rows[1]) * cols if count == 2 else rows[0] * cols
            analyse_lat(
                gh.at[i], xt.at[i], weight_ref, first, pq_f, pq_b, bd, wide,
                blocks, i * cols,
            )
            return carry

        lax.fori_loop(0, count, lat, 0)
        for k in range(0, members, 16):
            for h in range(cells // LANES):
                part = wide[h, k * blocks : (k + 16) * blocks, :].reshape(16, blocks, LANES)
                out_ref[k : k + 16, :, h * LANES : (h + 1) * LANES] = part.astype(BF16)

    any_spec = pl.BlockSpec(memory_space=pl.ANY)
    return pl.pallas_call(
        kernel,
        in_specs=[pl.BlockSpec(memory_space=pltpu.SMEM)] + [any_spec] * len(sources),
        out_specs=pl.BlockSpec(memory_space=pltpu.VMEM),
        out_shape=jax.ShapeDtypeStruct((members, blocks, cells), BF16),
        scratch_shapes=[
            pltpu.VMEM((count, 3, cols + 2, members + PAD, members), BF16),
            pltpu.VMEM((count, cols, members, cells), BF16),
            pltpu.VMEM((cols // 2, 2 * c, 2 * c), F32),
            pltpu.VMEM((cols // 2, 2 * c, 2 * c), BF16),
            pltpu.VMEM((cols // 2, 2 * c, 2 * c), BF16),
            pltpu.VMEM((cells // LANES, members * blocks, LANES), F32),
            pltpu.SemaphoreType.DMA((count,)),
        ],
        compiler_params=pltpu.CompilerParams(vmem_limit_bytes=VMEM_LIMIT),
        cost_estimate=pl.CostEstimate(
            flops=blocks * 2 * 14 * members**3,
            bytes_accessed=blocks * 4 * members * cells,
            transcendentals=0,
        ),
        name="analyse",
    )(weight, *sources)


def shift(value, axis, step, wrap):
    count = lax.axis_size(axis)
    pairs = [(i, (i + step) % count) for i in range(count) if wrap or 0 <= i + step < count]
    return lax.ppermute(value, axis, pairs)


def shards(members, obs_cell, obs_value, obs_rinv, obs_count, loc_pattern):
    mem_count = lax.axis_size("mem")
    blk_count = lax.axis_size("blk")
    devices = mem_count * blk_count
    lat_all, lon_all, cells = members.shape[1:]
    lat, lon = lat_all // mem_count, lon_all // blk_count
    slots = obs_cell.shape[2]

    live = lax.broadcasted_iota(jnp.int32, obs_rinv.shape, 2) < obs_count[:, :, None]
    root = jnp.sqrt(jnp.where(live, obs_rinv, 0.0))
    weight = (
        jnp.asarray(TAPER_WEIGHTS, F32) * loc_pattern.astype(F32)
    ).reshape(lat * lon * 9)

    grouped = members.reshape(mem_count, lat, blk_count, lon, cells).transpose(0, 2, 1, 3, 4)
    grouped = grouped.reshape(devices, lat * lon, cells)
    arrived = lax.all_to_all(grouped, AXES, split_axis=0, concat_axis=0, tiled=True)
    xt, gh = select(
        arrived,
        obs_cell.reshape(lat * lon, slots),
        obs_value.reshape(lat * lon, slots),
        root.reshape(lat * lon, slots),
    )
    rank = gh.shape[1:]
    xt = xt.reshape(lat, lon, devices, cells)
    gh = gh.reshape(lat, lon, *rank)
    west = shift(gh[:, lon - 1], "blk", 1, True)
    east = shift(gh[:, 0], "blk", -1, True)

    def full_row(r):
        return jnp.concatenate([west[r][None], gh[r], east[r][None]], axis=0)

    south = shift(full_row(lat - 1), "mem", 1, False)
    north = shift(full_row(0), "mem", -1, False)
    sources = [xt, gh, west, east, south, north]
    parts = []
    for r in range(0, lat, 2):
        rows = (r, r + 1)
        plan = []
        for row in rows:
            steps = [(0, row, "x", None)]
            for a in range(3):
                at = row + a - 1
                if at < 0:
                    steps.append((4, slice(None), (0, lon + 2), a))
                elif at >= lat:
                    steps.append((5, slice(None), (0, lon + 2), a))
                else:
                    steps.append((1, at, "own", a))
                    steps.append((2, pl.ds(at, 1), (0, 1), a))
                    steps.append((3, pl.ds(at, 1), (lon + 1, 1), a))
            plan.append(steps)
        parts.append(analyse(rows, weight, sources, plan, devices, lon, cells))
    result = jnp.concatenate(parts, axis=1)
    returned = lax.all_to_all(result, AXES, split_axis=0, concat_axis=0, tiled=True)
    returned = returned.reshape(mem_count, blk_count, lat, lon, cells).transpose(0, 2, 1, 3, 4)
    return returned.reshape(1, lat_all, lon_all, cells)


def solution(mesh):
    in_specs = (
        P(AXES, None, None, None),
        P("mem", "blk", None),
        P("mem", "blk", None),
        P("mem", "blk", None),
        P("mem", "blk"),
        P("mem", "blk", None),
    )
    out_specs = P(AXES, None, None, None)
    return jax.shard_map(shards, mesh=mesh, in_specs=in_specs, out_specs=out_specs, check_vma=False)
```

```python
import jax
import jax.numpy as jnp
from jax import lax
from jax.experimental import pallas as pl
from jax.experimental.pallas import tpu as pltpu
from jax.sharding import PartitionSpec as P

NS_STEPS = 5
TAPER_WEIGHTS = (0.3, 0.6, 0.3, 0.6, 1.0, 0.6, 0.3, 0.6, 0.3)
INFLATION = 1.1
F32 = jnp.float32
BF16 = jnp.bfloat16
PAD = 16
LANES = 128
AXES = ("mem", "blk")
VMEM_LIMIT = 62 * 1024 * 1024


def select(state, cell, value, root):
    members, _, cells = state.shape
    lat, cols, slots = cell.shape
    blocks = lat * cols
    group = 2 * cols
    pitch = group + 1

    def kernel(x_ref, cell_ref, value_ref, root_ref, xt_ref, gh_ref, first_ref, last_ref, wide, seen, left_ref):
        for k in range(members):
            part = x_ref[k].astype(F32)
            for h in range(cells // LANES):
                wide[h, k * pitch : k * pitch + group, :] = part[:, h * LANES : (h + 1) * LANES]
        ids = lax.broadcasted_iota(jnp.int32, (cells, slots), 0)
        pad_row = lax.broadcasted_iota(jnp.int32, (PAD, slots), 0)
        step = pl.program_id(0)

        def lat_row(half, carry):
            row = 2 * step + half
            means, lefts = [], []
            for j in range(cols):
                b = half * cols + j
                own = jnp.concatenate(
                    [
                        wide[h, pl.ds(b, members, stride=pitch), :].astype(BF16)
                        for h in range(cells // LANES)
                    ],
                    axis=1,
                )
                xt_ref[b] = own
                selector = (ids == cell_ref[row, j : j + 1, :]).astype(BF16)
                obs = jnp.dot(own, selector, preferred_element_type=F32)
                seen[j] = obs
                means.append(jnp.sum(obs, axis=0, keepdims=True) * (1.0 / members))
            for j in range(cols):
                scale = root_ref[row, j : j + 1, :]
                depart = (value_ref[row, j : j + 1, :] - means[j]) * scale
                high = depart.astype(BF16).astype(F32)
                extra = jnp.where(pad_row == 0, high, jnp.where(pad_row == 1, depart - high, 0.0))
                left_ref[j, :members] = ((seen[j] - means[j]) * scale).astype(BF16)
                left_ref[j, members:] = extra.astype(BF16)
            for j in range(cols):
                b = half * cols + j
                gram = lax.dot_general(
                    left_ref[j],
                    left_ref[j, :members],
                    (((1,), (1,)), ((), ())),
                    preferred_element_type=F32,
                )
                gain = gram[members : members + 1] + gram[members + 1 : members + 2]
                upper = gain.astype(BF16).astype(F32)
                tail = jnp.where(pad_row == 0, upper, jnp.where(pad_row == 1, gain - upper, 0.0))
                gram = gram[:members].astype(BF16)
                tail = tail.astype(BF16)
                targets = [gh_ref.at[b]]
                targets += [first_ref.at[half]] if j == 0 else []
                targets += [last_ref.at[half]] if j == cols - 1 else []
                for target in targets:
                    target[:members] = gram
                    target[members:] = tail
            return carry

        lax.fori_loop(0, 2, lat_row, 0)

    whole = pl.BlockSpec(cell.shape, lambda i: (0, 0, 0))
    edge = pl.BlockSpec((2, members + PAD, members), lambda i: (i, 0, 0))
    return pl.pallas_call(
        kernel,
        grid=(blocks // group,),
        in_specs=[
            pl.BlockSpec((members, group, cells), lambda i: (0, i, 0)),
            whole,
            whole,
            whole,
        ],
        out_specs=[
            pl.BlockSpec((group, members, cells), lambda i: (i, 0, 0)),
            pl.BlockSpec((group, members + PAD, members), lambda i: (i, 0, 0)),
            edge,
            edge,
        ],
        out_shape=[
            jax.ShapeDtypeStruct((blocks, members, cells), BF16),
            jax.ShapeDtypeStruct((blocks, members + PAD, members), BF16),
            jax.ShapeDtypeStruct((lat, members + PAD, members), BF16),
            jax.ShapeDtypeStruct((lat, members + PAD, members), BF16),
        ],
        scratch_shapes=[
            pltpu.VMEM((cells // LANES, members * pitch, LANES), F32),
            pltpu.VMEM((cols, members, slots), F32),
            pltpu.VMEM((cols, members + PAD, slots), BF16),
        ],
        compiler_params=pltpu.CompilerParams(vmem_limit_bytes=VMEM_LIMIT),
        cost_estimate=cost(blocks, 0.27),
        name="select",
    )(state, cell, value, root)


def cost(blocks, micros):
    return pl.CostEstimate(
        flops=int(blocks * micros * 1.1e9), bytes_accessed=blocks * 1000, transcendentals=0
    )


def interleave(main, other):
    done = 0
    for i, unit in enumerate(main):
        unit()
        while done < len(other) and done * len(main) < (i + 1) * len(other):
            other[done]()
            done += 1
    for unit in other[done:]:
        unit()


def combine_units(sites, base, gh, weight, cols, members, pq_f, pq_b, bd, norms, gains):
    ident = (
        lax.broadcasted_iota(jnp.int32, (members, members), 0)
        == lax.broadcasted_iota(jnp.int32, (members, members), 1)
    ).astype(F32)

    def unit(j, r, c):
        acc = None
        for n in range(9):
            term = gh[r - base[0] + n // 3, c - base[1] + n % 3].astype(F32)
            term = term * weight[(r * cols + c) * 9 + n]
            acc = term if acc is None else acc + term
        info = acc[:members] + (members - 1) / INFLATION * ident
        gains[r, c] = acc[members : members + 1] + acc[members + 1 : members + 2]
        inv = lax.rsqrt(jnp.sum(jnp.sum(info * info, axis=0, keepdims=True), axis=1, keepdims=True))
        norms[r, c] = inv
        p = info * inv
        third = p * (1.0 / 3.0)
        q = ident - third
        pq_f[j, :members] = p
        pq_b[j, :members] = p.astype(BF16)
        pq_f[j, members:] = q
        pq_b[j, members:] = q.astype(BF16)
        bd[j] = third.astype(BF16)

    return [lambda j=j, r=r, c=c: unit(j, r, c) for j, (r, c) in enumerate(sites)]


def newton_units(count, members, pq_f, pq_b, bd):
    c = members

    def opening(j):
        p = pq_f[j, :c] - jnp.dot(pq_b[j, :c], bd[j], preferred_element_type=F32)
        pq_f[j, :c] = p
        pq_b[j, :c] = p.astype(BF16)

    def product(j, step):
        scale = 1.5 ** (2 * step) / 3.0
        prod = jnp.dot(pq_b[j, c:], pq_b[j, :c], preferred_element_type=F32)
        bd[j] = (prod * scale).astype(BF16)

    def update(j, step):
        start = 0 if step < NS_STEPS - 1 else c
        new = pq_f[j, start:] - jnp.dot(pq_b[j, start:], bd[j], preferred_element_type=F32)
        pq_f[j, start:] = new
        if start == 0:
            pq_b[j] = new.astype(BF16)

    units = [lambda j=j: opening(j) for j in range(count)]
    for step in range(1, NS_STEPS):
        for part in (product, update):
            units += [lambda j=j, step=step, part=part: part(j, step) for j in range(count)]
    return units


def transform_of(j, site, members, pq_f, norms, gains):
    q = pq_f[j, members:] * 1.5**NS_STEPS
    inv = norms[site]
    column = jnp.sum(q * gains[site], axis=1, keepdims=True)
    weights_row = jnp.sum(q * column, axis=0, keepdims=True) * inv
    return (q * jnp.sqrt((members - 1.0) * inv) + weights_row).astype(BF16)


def inner_transforms(gh, weight, sites, first, depth, members, cols):
    c = members
    most = max(map(len, sites))
    total = sum(map(len, sites))

    def kernel(weight_ref, gh_ref, out_ref, held, pq_f, pq_b, bd, sem):
        def fetch(i):
            return pltpu.make_async_copy(gh_ref.at[first + i], held.at[i], sem.at[i])

        for i in range(depth):
            fetch(i).start()
        norms, gains = {}, {}

        def combine(g):
            two = g % 2
            return combine_units(
                sites[g], (first + 1, 1), held, weight_ref, cols, members,
                pq_f.at[two], pq_b.at[two], bd.at[two], norms, gains,
            )

        def finish(g):
            at = sum(map(len, sites[:g]))

            def unit(j, site):
                out_ref[at + j] = transform_of(j, site, members, pq_f.at[g % 2], norms, gains)

            return [lambda j=j, site=site: unit(j, site) for j, site in enumerate(sites[g])]

        for i in range(depth - len(sites) + 1):
            fetch(i).wait()
        interleave(combine(0), [])
        for g in range(len(sites)):
            beside = finish(g - 1) if g else []
            if g + 1 < len(sites):
                fetch(depth - len(sites) + 1 + g).wait()
                beside = beside + combine(g + 1)
            two = g % 2
            units = newton_units(len(sites[g]), members, pq_f.at[two], pq_b.at[two], bd.at[two])
            interleave(units, beside)
        interleave(finish(len(sites) - 1), [])

    return pl.pallas_call(
        kernel,
        in_specs=[pl.BlockSpec(memory_space=pltpu.SMEM), pl.BlockSpec(memory_space=pl.ANY)],
        out_specs=pl.BlockSpec(memory_space=pltpu.VMEM),
        out_shape=jax.ShapeDtypeStruct((total, members, members), BF16),
        scratch_shapes=[
            pltpu.VMEM((depth, cols, members + PAD, members), BF16),
            pltpu.VMEM((2, most, 2 * c, c), F32),
            pltpu.VMEM((2, most, 2 * c, c), BF16),
            pltpu.VMEM((2, most, c, c), BF16),
            pltpu.SemaphoreType.DMA((depth,)),
        ],
        compiler_params=pltpu.CompilerParams(vmem_limit_bytes=VMEM_LIMIT),
        cost_estimate=cost(total, 0.4),
        name="inner_transforms",
    )(weight, gh)


def analyse(weight, gh, west, east, south, north, xt, ready, ready_sites):
    lat, cols, tall, members = gh.shape
    cells = xt.shape[2]
    c = members
    pitch = 2 * cols + 1
    pairs = lat // 2
    site_of = {site: i for ref, sites in enumerate(ready_sites) for i, site in enumerate(sites)}
    array_of = {site: ref for ref, sites in enumerate(ready_sites) for site in sites}
    rim = [[(r, k) for r in range(lat) for k in range(cols) if (r, k) not in site_of and p(r)]
           for p in (lambda r: 2 <= r < lat - 2, lambda r: r < 2, lambda r: r >= lat - 2)]
    most = max(map(len, rim))
    middle = list(range(1, pairs - 1))
    finished = [middle, [0], [pairs - 1]]

    def kernel(*refs):
        weight_ref, gh_ref, west_ref, east_ref, south_ref, north_ref, xt_ref = refs[:7]
        ready_refs = refs[7 : 7 + len(ready)]
        (out_ref, held, states, kept_a, kept_b, pq_f, pq_b, bd, wide, narrow,
         row_sem, state_sem, kept_sem, out_sem) = refs[7 + len(ready) :]
        kept = (kept_a, kept_b)

        def copy(src, dst, sem):
            pltpu.make_async_copy(src, dst, sem).start()

        for r in list(range(1, lat - 1)) + [0, lat - 1]:
            copy(gh_ref.at[r], held.at[r + 1, pl.ds(1, cols)], row_sem.at[r + 1])
            copy(west_ref.at[pl.ds(r, 1)], held.at[r + 1, pl.ds(0, 1)], row_sem.at[r + 1])
            copy(east_ref.at[pl.ds(r, 1)], held.at[r + 1, pl.ds(cols + 1, 1)], row_sem.at[r + 1])
        for src, dst, sem in zip(ready_refs, kept, (0, 1)):
            copy(src, dst, kept_sem.at[sem])
        for pair in middle + [0, pairs - 1]:
            span = pl.ds(pair * 2 * cols, 2 * cols)
            copy(xt_ref.at[span], states.at[span], state_sem.at[pair])
        copy(south_ref, held.at[0], row_sem.at[0])
        copy(north_ref, held.at[lat + 1], row_sem.at[lat + 1])

        def rows_in(*which):
            for r in which:
                pltpu.make_async_copy(held.at[r], held.at[r], row_sem.at[r]).wait()

        def states_in(*which):
            for pair in which:
                span = pl.ds(pair * 2 * cols, 2 * cols)
                pltpu.make_async_copy(states.at[span], states.at[span], state_sem.at[pair]).wait()

        norms, gains = {}, {}

        def combine(g):
            two = g % 2
            return combine_units(
                rim[g], (0, 0), held, weight_ref, cols, members,
                pq_f.at[two], pq_b.at[two], bd.at[two], norms, gains,
            )

        def apply(r, k, transform):
            ones = jnp.full((PAD, members), 1.0 / members, BF16)
            rest = 1.0 - jnp.sum(transform.astype(F32), axis=1, keepdims=True)
            left = jnp.concatenate([transform, ones], axis=0)
            out = jnp.dot(left, states[r * cols + k], preferred_element_type=F32)
            out = out[:members] + rest * out[members : members + 1]
            for h in range(cells // LANES):
                wide[r // 2, h, pl.ds(r % 2 * cols + k, members, stride=pitch), :] = (
                    out[:, h * LANES : (h + 1) * LANES]
                )

        def inner(which):
            sites = [site for site in site_of if site[0] // 2 in which]
            return [
                lambda s=s: apply(*s, kept[array_of[s]][site_of[s]]) for s in sites
            ]

        def finish(g):
            return [
                lambda j=j, s=s: apply(
                    *s, transform_of(j, s, members, pq_f.at[g % 2], norms, gains)
                )
                for j, s in enumerate(rim[g])
            ]

        def sent(pair):
            return pltpu.make_async_copy(
                narrow.at[pair], out_ref.at[:, pl.ds(pair * 2 * cols, 2 * cols)],
                out_sem.at[pair],
            )

        def convert(pair):
            def unit(start):
                for k in range(start, start + members // 8):
                    for h in range(cells // LANES):
                        part = wide[pair, h, k * pitch : k * pitch + 2 * cols, :]
                        narrow[pair, k, :, h * LANES : (h + 1) * LANES] = part.astype(BF16)

            units = [lambda k=k: unit(k) for k in range(0, members, members // 8)]
            return units + [lambda: sent(pair).start()]

        def newton(g):
            two = g % 2
            return newton_units(len(rim[g]), members, pq_f.at[two], pq_b.at[two], bd.at[two])

        rows_in(*range(2, lat))
        interleave(combine(0), [])
        for i in range(len(ready)):
            pltpu.make_async_copy(kept[i], kept[i], kept_sem.at[i]).wait()
        states_in(*middle)
        rows_in(0, 1)
        interleave(newton(0), combine(1) + inner(middle))
        rows_in(lat, lat + 1)
        states_in(0, pairs - 1)
        beside = finish(0) + combine(2)
        for pair in middle:
            beside = beside + convert(pair)
        interleave(newton(1), beside + inner([0]))
        interleave(newton(2), finish(1) + convert(0) + inner([pairs - 1]))
        interleave(finish(2) + convert(pairs - 1), [])
        for pair in range(pairs):
            sent(pair).wait()

    any_spec = pl.BlockSpec(memory_space=pl.ANY)
    return pl.pallas_call(
        kernel,
        in_specs=[pl.BlockSpec(memory_space=pltpu.SMEM)] + [any_spec] * (6 + len(ready)),
        out_specs=any_spec,
        out_shape=jax.ShapeDtypeStruct((members, lat * cols, cells), BF16),
        scratch_shapes=[
            pltpu.VMEM((lat + 2, cols + 2, tall, members), BF16),
            pltpu.VMEM(xt.shape, BF16),
            pltpu.VMEM(ready[0].shape, BF16),
            pltpu.VMEM(ready[1].shape, BF16),
            pltpu.VMEM((2, most, 2 * c, c), F32),
            pltpu.VMEM((2, most, 2 * c, c), BF16),
            pltpu.VMEM((2, most, c, c), BF16),
            pltpu.VMEM((pairs, cells // LANES, members * pitch, LANES), F32),
            pltpu.VMEM((pairs, members, 2 * cols, cells), BF16),
            pltpu.SemaphoreType.DMA((lat + 2,)),
            pltpu.SemaphoreType.DMA((pairs,)),
            pltpu.SemaphoreType.DMA((2,)),
            pltpu.SemaphoreType.DMA((pairs,)),
        ],
        compiler_params=pltpu.CompilerParams(vmem_limit_bytes=VMEM_LIMIT),
        cost_estimate=cost(lat * cols, 0.25),
        name="analyse",
    )(weight, gh, west, east, south, north, xt, *ready)


def shift(value, axis, step, wrap):
    count = lax.axis_size(axis)
    pairs = [(i, (i + step) % count) for i in range(count) if wrap or 0 <= i + step < count]
    return lax.ppermute(value, axis, pairs)


def shards(members, obs_cell, obs_value, obs_rinv, obs_count, loc_pattern):
    mem_count = lax.axis_size("mem")
    blk_count = lax.axis_size("blk")
    devices = mem_count * blk_count
    lat_all, lon_all, cells = members.shape[1:]
    lat, lon = lat_all // mem_count, lon_all // blk_count
    slots = obs_cell.shape[2]

    live = lax.broadcasted_iota(jnp.int32, obs_rinv.shape, 2) < obs_count[:, :, None]
    root = jnp.sqrt(jnp.where(live, obs_rinv, 0.0))
    weight = (
        jnp.asarray(TAPER_WEIGHTS, F32) * loc_pattern.astype(F32)
    ).reshape(lat * lon * 9)

    tiled = members.reshape(mem_count, lat, blk_count, lon, cells).transpose(0, 2, 1, 3, 4)
    arrived = lax.all_to_all(
        tiled.reshape(devices, lat * lon, cells), AXES, split_axis=0, concat_axis=0, tiled=True
    )
    xt, gh, first, last = select(arrived, obs_cell, obs_value, root)
    gh = gh.reshape(lat, lon, *gh.shape[1:])
    west = shift(last, "blk", 1, True)
    east = shift(first, "blk", -1, True)
    half = lat // 2
    inner = [
        [[(r, c) for c in range(1, lon - 1)] for r in rows]
        for rows in (range(1, half), range(half, lat - 1))
    ]
    ready = [
        inner_transforms(gh, weight, sites, start, half + 1, devices, lon)
        for sites, start in zip(inner, (0, half - 1))
    ]

    def full_row(r):
        return jnp.concatenate([west[r][None], gh[r], east[r][None]], axis=0)

    south = shift(full_row(lat - 1), "mem", 1, False)
    north = shift(full_row(0), "mem", -1, False)
    result = analyse(
        weight, gh, west, east, south, north, xt, ready, [sum(sites, []) for sites in inner]
    )
    back = lax.all_to_all(result, AXES, split_axis=0, concat_axis=0, tiled=True)
    back = back.reshape(mem_count, blk_count, lat, lon, cells).transpose(0, 2, 1, 3, 4)
    return back.reshape(1, lat_all, lon_all, cells)


def solution(mesh):
    in_specs = (
        P(AXES, None, None, None),
        P("mem", "blk", None),
        P("mem", "blk", None),
        P("mem", "blk", None),
        P("mem", "blk"),
        P("mem", "blk", None),
    )
    out_specs = P(AXES, None, None, None)
    return jax.shard_map(shards, mesh=mesh, in_specs=in_specs, out_specs=out_specs, check_vma=False)
```

```python
import jax
import jax.numpy as jnp
from jax import lax
from jax.experimental import pallas as pl
from jax.experimental.pallas import tpu as pltpu
from jax.sharding import PartitionSpec as P

NS_STEPS = 5
TAPER_WEIGHTS = (0.3, 0.6, 0.3, 0.6, 1.0, 0.6, 0.3, 0.6, 0.3)
INFLATION = 1.1
F32 = jnp.float32
BF16 = jnp.bfloat16
PAD = 16
LANES = 128
AXES = ("mem", "blk")
VMEM_LIMIT = 62 * 1024 * 1024


def select(state, cell, value, rinv, live):
    members, _, cells = state.shape
    lat, cols, slots = cell.shape
    blocks = lat * cols
    group = 2 * cols
    pitch = group + 1

    def kernel(x_ref, cell_ref, value_ref, rinv_ref, live_ref, xt_ref, gh_ref, first_ref, last_ref, wide, seen, left_ref):
        for k in range(members):
            part = x_ref[k].astype(F32)
            for h in range(cells // LANES):
                wide[h, k * pitch : k * pitch + group, :] = part[:, h * LANES : (h + 1) * LANES]
        ids = lax.broadcasted_iota(jnp.int32, (cells, slots), 0)
        pad_row = lax.broadcasted_iota(jnp.int32, (PAD, slots), 0)
        slot = lax.broadcasted_iota(jnp.int32, (1, slots), 1)
        step = pl.program_id(0)

        def lat_row(half, carry):
            row = 2 * step + half
            means, lefts = [], []
            for j in range(cols):
                b = half * cols + j
                own = jnp.concatenate(
                    [
                        wide[h, pl.ds(b, members, stride=pitch), :].astype(BF16)
                        for h in range(cells // LANES)
                    ],
                    axis=1,
                )
                xt_ref[b] = own
                selector = (ids == cell_ref[row, j : j + 1, :]).astype(BF16)
                obs = jnp.dot(own, selector, preferred_element_type=F32)
                seen[j] = obs
                means.append(jnp.sum(obs, axis=0, keepdims=True) * (1.0 / members))
            for j in range(cols):
                weight = jnp.where(slot < live_ref[row, j], rinv_ref[row, j : j + 1, :], 0.0)
                scale = jnp.sqrt(weight)
                depart = (value_ref[row, j : j + 1, :] - means[j]) * scale
                high = depart.astype(BF16).astype(F32)
                extra = jnp.where(pad_row == 0, high, jnp.where(pad_row == 1, depart - high, 0.0))
                left_ref[j, :members] = ((seen[j] - means[j]) * scale).astype(BF16)
                left_ref[j, members:] = extra.astype(BF16)
            for j in range(cols):
                b = half * cols + j
                gram = lax.dot_general(
                    left_ref[j],
                    left_ref[j, :members],
                    (((1,), (1,)), ((), ())),
                    preferred_element_type=F32,
                )
                gain = gram[members : members + 1] + gram[members + 1 : members + 2]
                upper = gain.astype(BF16).astype(F32)
                tail = jnp.where(pad_row == 0, upper, jnp.where(pad_row == 1, gain - upper, 0.0))
                gram = gram[:members].astype(BF16)
                tail = tail.astype(BF16)
                targets = [gh_ref.at[b]]
                targets += [first_ref.at[half]] if j == 0 else []
                targets += [last_ref.at[half]] if j == cols - 1 else []
                for target in targets:
                    target[:members] = gram
                    target[members:] = tail
            return carry

        lax.fori_loop(0, 2, lat_row, 0)

    whole = pl.BlockSpec(cell.shape, lambda i: (0, 0, 0))
    edge = pl.BlockSpec((2, members + PAD, members), lambda i: (i, 0, 0))
    return pl.pallas_call(
        kernel,
        grid=(blocks // group,),
        in_specs=[
            pl.BlockSpec((members, group, cells), lambda i: (0, i, 0)),
            whole,
            whole,
            whole,
            pl.BlockSpec(memory_space=pltpu.SMEM),
        ],
        out_specs=[
            pl.BlockSpec((group, members, cells), lambda i: (i, 0, 0)),
            pl.BlockSpec((group, members + PAD, members), lambda i: (i, 0, 0)),
            edge,
            edge,
        ],
        out_shape=[
            jax.ShapeDtypeStruct((blocks, members, cells), BF16),
            jax.ShapeDtypeStruct((blocks, members + PAD, members), BF16),
            jax.ShapeDtypeStruct((lat, members + PAD, members), BF16),
            jax.ShapeDtypeStruct((lat, members + PAD, members), BF16),
        ],
        scratch_shapes=[
            pltpu.VMEM((cells // LANES, members * pitch, LANES), F32),
            pltpu.VMEM((cols, members, slots), F32),
            pltpu.VMEM((cols, members + PAD, slots), BF16),
        ],
        compiler_params=pltpu.CompilerParams(vmem_limit_bytes=VMEM_LIMIT),
        cost_estimate=cost(blocks, 0.27),
        name="select",
    )(state, cell, value, rinv, live)


def cost(blocks, micros):
    return pl.CostEstimate(
        flops=int(blocks * micros * 1.1e9), bytes_accessed=blocks * 1000, transcendentals=0
    )


def interleave(main, other):
    done = 0
    for i, unit in enumerate(main):
        unit()
        while done < len(other) and done * len(main) < (i + 1) * len(other):
            other[done]()
            done += 1
    for unit in other[done:]:
        unit()


def combine_units(sites, base, gh, pattern, cols, members, pq_f, pq_b, bd, norms, gains):
    ident = (
        lax.broadcasted_iota(jnp.int32, (members, members), 0)
        == lax.broadcasted_iota(jnp.int32, (members, members), 1)
    ).astype(F32)

    def unit(j, r, c):
        acc = None
        for n in range(9):
            term = gh[r - base[0] + n // 3, c - base[1] + n % 3].astype(F32)
            term = term * (TAPER_WEIGHTS[n] * pattern[r, c, n].astype(F32))
            acc = term if acc is None else acc + term
        info = acc[:members] + (members - 1) / INFLATION * ident
        gains[r, c] = acc[members : members + 1] + acc[members + 1 : members + 2]
        inv = lax.rsqrt(jnp.sum(jnp.sum(info * info, axis=0, keepdims=True), axis=1, keepdims=True))
        norms[r, c] = inv
        p = info * inv
        third = p * (1.0 / 3.0)
        q = ident - third
        pq_f[j, :members] = p
        pq_b[j, :members] = p.astype(BF16)
        pq_f[j, members:] = q
        pq_b[j, members:] = q.astype(BF16)
        bd[j] = third.astype(BF16)

    return [lambda j=j, r=r, c=c: unit(j, r, c) for j, (r, c) in enumerate(sites)]


def newton_units(count, members, pq_f, pq_b, bd):
    c = members

    def opening(j):
        p = pq_f[j, :c] - jnp.dot(pq_b[j, :c], bd[j], preferred_element_type=F32)
        pq_f[j, :c] = p
        pq_b[j, :c] = p.astype(BF16)

    def product(j, step):
        scale = 1.5 ** (2 * step) / 3.0
        prod = jnp.dot(pq_b[j, c:], pq_b[j, :c], preferred_element_type=F32)
        bd[j] = (prod * scale).astype(BF16)

    def update(j, step):
        start = 0 if step < NS_STEPS - 1 else c
        new = pq_f[j, start:] - jnp.dot(pq_b[j, start:], bd[j], preferred_element_type=F32)
        pq_f[j, start:] = new
        if start == 0:
            pq_b[j] = new.astype(BF16)

    units = [lambda j=j: opening(j) for j in range(count)]
    for step in range(1, NS_STEPS):
        for part in (product, update):
            units += [lambda j=j, step=step, part=part: part(j, step) for j in range(count)]
    return units


def transform_of(j, site, members, pq_f, norms, gains):
    q = pq_f[j, members:] * 1.5**NS_STEPS
    inv = norms[site]
    column = jnp.sum(q * gains[site], axis=1, keepdims=True)
    weights_row = jnp.sum(q * column, axis=0, keepdims=True) * inv
    return (q * jnp.sqrt((members - 1.0) * inv) + weights_row).astype(BF16)


def inner_transforms(gh, pattern, sites, first, depth, members, cols):
    c = members
    most = max(map(len, sites))
    total = sum(map(len, sites))

    def kernel(pattern_ref, gh_ref, out_ref, held, pq_f, pq_b, bd, sem):
        def fetch(i):
            return pltpu.make_async_copy(gh_ref.at[first + i], held.at[i], sem.at[i])

        for i in range(depth):
            fetch(i).start()
        norms, gains = {}, {}

        def combine(g):
            two = g % 2
            return combine_units(
                sites[g], (first + 1, 1), held, pattern_ref, cols, members,
                pq_f.at[two], pq_b.at[two], bd.at[two], norms, gains,
            )

        def finish(g):
            at = sum(map(len, sites[:g]))

            def unit(j, site):
                out_ref[at + j] = transform_of(j, site, members, pq_f.at[g % 2], norms, gains)

            return [lambda j=j, site=site: unit(j, site) for j, site in enumerate(sites[g])]

        for i in range(depth - len(sites) + 1):
            fetch(i).wait()
        interleave(combine(0), [])
        for g in range(len(sites)):
            beside = finish(g - 1) if g else []
            if g + 1 < len(sites):
                fetch(depth - len(sites) + 1 + g).wait()
                beside = beside + combine(g + 1)
            two = g % 2
            units = newton_units(len(sites[g]), members, pq_f.at[two], pq_b.at[two], bd.at[two])
            interleave(units, beside)
        interleave(finish(len(sites) - 1), [])

    return pl.pallas_call(
        kernel,
        in_specs=[pl.BlockSpec(memory_space=pltpu.SMEM), pl.BlockSpec(memory_space=pl.ANY)],
        out_specs=pl.BlockSpec(memory_space=pltpu.VMEM),
        out_shape=jax.ShapeDtypeStruct((total, members, members), BF16),
        scratch_shapes=[
            pltpu.VMEM((depth, cols, members + PAD, members), BF16),
            pltpu.VMEM((2, most, 2 * c, c), F32),
            pltpu.VMEM((2, most, 2 * c, c), BF16),
            pltpu.VMEM((2, most, c, c), BF16),
            pltpu.SemaphoreType.DMA((depth,)),
        ],
        compiler_params=pltpu.CompilerParams(vmem_limit_bytes=VMEM_LIMIT),
        cost_estimate=cost(total, 0.4),
        name="inner_transforms",
    )(pattern, gh)


def analyse(pattern, gh, west, east, beyond, xt, pairs, groups, ready, ready_sites):
    lat, cols, tall, members = gh.shape
    cells = xt.shape[2]
    c = members
    pitch = 2 * cols + 1
    most = max(map(len, groups))
    span = 2 * cols
    last_of = {p: max(g for g, sites in enumerate(groups) for r, _ in sites if r // 2 == p)
               for p in pairs}
    slot = {p: i for i, p in enumerate(pairs)}
    needed = [sorted({r + a for r, _ in sites for a in range(3)}) for sites in groups]
    fresh = [[r for r in rows if all(r not in old for old in needed[:g])]
             for g, rows in enumerate(needed)]
    sources = [pattern, gh, west, east, xt, *beyond, *ready]
    starts = [sum(map(len, ready_sites[:i])) for i in range(len(ready_sites))]

    def kernel(*refs):
        pattern_ref, gh_ref, west_ref, east_ref, xt_ref = refs[:5]
        beyond_refs = refs[5 : 5 + len(beyond)]
        ready_refs = refs[5 + len(beyond) : len(sources)]
        (out_ref, held, states, kept, pq_f, pq_b, bd, wide, narrow,
         row_sem, state_sem, kept_sem, out_sem) = refs[len(sources) :]

        def copy(src, dst, sem):
            pltpu.make_async_copy(src, dst, sem).start()

        for g, rows in enumerate(fresh):
            for r in rows:
                if r in (0, lat + 1):
                    copy(beyond_refs[r // (lat + 1)], held.at[r], row_sem.at[r])
                    continue
                copy(gh_ref.at[r - 1], held.at[r, pl.ds(1, cols)], row_sem.at[r])
                copy(west_ref.at[pl.ds(r - 1, 1)], held.at[r, pl.ds(0, 1)], row_sem.at[r])
                copy(east_ref.at[pl.ds(r - 1, 1)], held.at[r, pl.ds(cols + 1, 1)], row_sem.at[r])
            if g == 0:
                for i, ref in enumerate(ready_refs):
                    copy(ref, kept.at[pl.ds(starts[i], ref.shape[0])], kept_sem.at[i])
                for p in pairs:
                    copy(xt_ref.at[pl.ds(p * span, span)], states.at[slot[p]],
                         state_sem.at[slot[p]])

        def rows_in(g):
            for r in fresh[g]:
                pltpu.make_async_copy(held.at[r], held.at[r], row_sem.at[r]).wait()

        norms, gains = {}, {}

        def combine(g):
            two = g % 2
            return combine_units(
                groups[g], (0, 0), held, pattern_ref, cols, members,
                pq_f.at[two], pq_b.at[two], bd.at[two], norms, gains,
            )

        def apply(r, k, transform):
            ones = jnp.full((PAD, members), 1.0 / members, BF16)
            rest = 1.0 - jnp.sum(transform.astype(F32), axis=1, keepdims=True)
            left = jnp.concatenate([transform, ones], axis=0)
            at = r % 2 * cols + k
            out = jnp.dot(left, states[slot[r // 2], at], preferred_element_type=F32)
            out = out[:members] + rest * out[members : members + 1]
            for h in range(cells // LANES):
                wide[slot[r // 2], h, pl.ds(at, members, stride=pitch), :] = (
                    out[:, h * LANES : (h + 1) * LANES]
                )

        def finish(g):
            units = [
                lambda j=j, s=s: apply(
                    *s, transform_of(j, s, members, pq_f.at[g % 2], norms, gains)
                )
                for j, s in enumerate(groups[g])
            ]
            for p in pairs:
                if last_of[p] == g:
                    units += convert(slot[p])
            return units

        def sent(i):
            return pltpu.make_async_copy(
                narrow.at[i], out_ref.at[:, pl.ds(i * span, span)], out_sem.at[i]
            )

        def convert(i):
            def unit(start):
                for k in range(start, start + members // 8):
                    for h in range(cells // LANES):
                        part = wide[i, h, k * pitch : k * pitch + span, :]
                        narrow[i, k, :, h * LANES : (h + 1) * LANES] = part.astype(BF16)

            units = [lambda k=k: unit(k) for k in range(0, members, members // 8)]
            return units + [lambda: sent(i).start()]

        rows_in(0)
        interleave(combine(0), [])
        for i, ref in enumerate(ready_refs):
            part = kept.at[pl.ds(starts[i], ref.shape[0])]
            pltpu.make_async_copy(part, part, kept_sem.at[i]).wait()
        for p in pairs:
            i = slot[p]
            pltpu.make_async_copy(states.at[i], states.at[i], state_sem.at[i]).wait()
        for g in range(len(groups)):
            beside = finish(g - 1) if g else []
            beside = beside + [
                lambda i=i, s=s: apply(*s, kept[i])
                for i, s in enumerate(ready_sites[g], starts[g])
            ]
            if g + 1 < len(groups):
                rows_in(g + 1)
                beside = beside + combine(g + 1)
            two = g % 2
            units = newton_units(len(groups[g]), members, pq_f.at[two], pq_b.at[two], bd.at[two])
            interleave(units, beside)
        interleave(finish(len(groups) - 1), [])
        for p in pairs:
            sent(slot[p]).wait()

    any_spec = pl.BlockSpec(memory_space=pl.ANY)
    count = len(pairs)
    return pl.pallas_call(
        kernel,
        in_specs=[pl.BlockSpec(memory_space=pltpu.SMEM)] + [any_spec] * (len(sources) - 1),
        out_specs=any_spec,
        out_shape=jax.ShapeDtypeStruct((members, count * span, cells), BF16),
        scratch_shapes=[
            pltpu.VMEM((lat + 2, cols + 2, tall, members), BF16),
            pltpu.VMEM((count, span, members, cells), BF16),
            pltpu.VMEM((sum(map(len, ready_sites)), members, members), BF16),
            pltpu.VMEM((2, most, 2 * c, c), F32),
            pltpu.VMEM((2, most, 2 * c, c), BF16),
            pltpu.VMEM((2, most, c, c), BF16),
            pltpu.VMEM((count, cells // LANES, members * pitch, LANES), F32),
            pltpu.VMEM((count, members, span, cells), BF16),
            pltpu.SemaphoreType.DMA((lat + 2,)),
            pltpu.SemaphoreType.DMA((count,)),
            pltpu.SemaphoreType.DMA((len(ready),)),
            pltpu.SemaphoreType.DMA((count,)),
        ],
        compiler_params=pltpu.CompilerParams(vmem_limit_bytes=VMEM_LIMIT),
        cost_estimate=cost(count * span, 0.35),
        name="analyse",
    )(*sources)


def shift(value, axis, step, wrap):
    count = lax.axis_size(axis)
    pairs = [(i, (i + step) % count) for i in range(count) if wrap or 0 <= i + step < count]
    return lax.ppermute(value, axis, pairs)


def shards(members, obs_cell, obs_value, obs_rinv, obs_count, loc_pattern):
    mem_count = lax.axis_size("mem")
    blk_count = lax.axis_size("blk")
    devices = mem_count * blk_count
    lat_all, lon_all, cells = members.shape[1:]
    lat, lon = lat_all // mem_count, lon_all // blk_count
    slots = obs_cell.shape[2]

    tiled = members.reshape(mem_count, lat, blk_count, lon, cells).transpose(0, 2, 1, 3, 4)
    arrived = lax.all_to_all(
        tiled.reshape(devices, lat * lon, cells), AXES, split_axis=0, concat_axis=0, tiled=True
    )
    xt, gh, first, last = select(arrived, obs_cell, obs_value, obs_rinv, obs_count)
    gh = gh.reshape(lat, lon, *gh.shape[1:])
    west = shift(last, "blk", 1, True)
    east = shift(first, "blk", -1, True)
    half = lat // 2
    inner = [
        [(r, c) for r in rows for c in range(1, lon - 1)]
        for rows in (range(1, half), range(half, lat - 1))
    ]
    ready = [
        inner_transforms(gh, loc_pattern, [sites], start, half + 1, devices, lon)
        for sites, start in zip(inner, (0, half - 1))
    ]
    rim = [
        [(r, c) for r in rows for c in range(lon) if (r, c) not in inner[0] + inner[1]]
        for rows in (range(half), range(half, lat))
    ]

    def full_row(r):
        return jnp.concatenate([west[r][None], gh[r], east[r][None]], axis=0)

    south = shift(full_row(lat - 1), "mem", 1, False)
    north = shift(full_row(0), "mem", -1, False)
    result = analyse(
        loc_pattern, gh, west, east, [south, north], xt, tuple(range(half)), rim, ready, inner
    )
    back = lax.all_to_all(result, AXES, split_axis=0, concat_axis=0, tiled=True)
    back = back.reshape(mem_count, blk_count, lat, lon, cells).transpose(0, 2, 1, 3, 4)
    return back.reshape(1, lat_all, lon_all, cells)


def solution(mesh):
    in_specs = (
        P(AXES, None, None, None),
        P("mem", "blk", None),
        P("mem", "blk", None),
        P("mem", "blk", None),
        P("mem", "blk"),
        P("mem", "blk", None),
    )
    out_specs = P(AXES, None, None, None)
    return jax.shard_map(shards, mesh=mesh, in_specs=in_specs, out_specs=out_specs, check_vma=False)
```

```python
import jax
import jax.numpy as jnp
from jax import lax
from jax.experimental import pallas as pl
from jax.experimental.pallas import tpu as pltpu
from jax.sharding import PartitionSpec as P

NS_STEPS = 5
TAPER_WEIGHTS = (0.3, 0.6, 0.3, 0.6, 1.0, 0.6, 0.3, 0.6, 0.3)
INFLATION = 1.1
F32 = jnp.float32
BF16 = jnp.bfloat16
PAD = 16
LANES = 128
AXES = ("mem", "blk")
VMEM_LIMIT = 62 * 1024 * 1024


def select(state, cell, value, rinv, live):
    members, _, cells = state.shape
    lat, cols, slots = cell.shape
    blocks = lat * cols
    group = 2 * cols
    pitch = group + 1

    def kernel(x_ref, cell_ref, value_ref, rinv_ref, live_ref, xt_ref, gh_ref, first_ref, last_ref, wide, seen, left_ref):
        for k in range(members):
            part = x_ref[k].astype(F32)
            for h in range(cells // LANES):
                wide[h, k * pitch : k * pitch + group, :] = part[:, h * LANES : (h + 1) * LANES]
        ids = lax.broadcasted_iota(jnp.int32, (cells, slots), 0)
        pad_row = lax.broadcasted_iota(jnp.int32, (PAD, slots), 0)
        slot = lax.broadcasted_iota(jnp.int32, (1, slots), 1)
        step = pl.program_id(0)

        means = []
        for b in range(2 * cols):
            half, j = divmod(b, cols)
            row = 2 * step + half
            own = jnp.concatenate(
                [
                    wide[h, pl.ds(b, members, stride=pitch), :].astype(BF16)
                    for h in range(cells // LANES)
                ],
                axis=1,
            )
            xt_ref[b] = own
            selector = (ids == cell_ref[row, j : j + 1, :]).astype(BF16)
            obs = jnp.dot(own, selector, preferred_element_type=F32)
            seen[b] = obs
            means.append(jnp.sum(obs, axis=0, keepdims=True) * (1.0 / members))
        for b in range(2 * cols):
            half, j = divmod(b, cols)
            row = 2 * step + half
            weight = jnp.where(slot < live_ref[row, j], rinv_ref[row, j : j + 1, :], 0.0)
            scale = jnp.sqrt(weight)
            depart = (value_ref[row, j : j + 1, :] - means[b]) * scale
            high = depart.astype(BF16).astype(F32)
            extra = jnp.where(pad_row == 0, high, jnp.where(pad_row == 1, depart - high, 0.0))
            left_ref[b, :members] = ((seen[b] - means[b]) * scale).astype(BF16)
            left_ref[b, members:] = extra.astype(BF16)
        for b in range(2 * cols):
            half, j = divmod(b, cols)
            gram = lax.dot_general(
                left_ref[b],
                left_ref[b, :members],
                (((1,), (1,)), ((), ())),
                preferred_element_type=F32,
            )
            gain = gram[members : members + 1] + gram[members + 1 : members + 2]
            upper = gain.astype(BF16).astype(F32)
            tail = jnp.where(pad_row == 0, upper, jnp.where(pad_row == 1, gain - upper, 0.0))
            gram = gram[:members].astype(BF16)
            tail = tail.astype(BF16)
            targets = [gh_ref.at[b]]
            targets += [first_ref.at[half]] if j == 0 else []
            targets += [last_ref.at[half]] if j == cols - 1 else []
            for target in targets:
                target[:members] = gram
                target[members:] = tail

    whole = pl.BlockSpec(cell.shape, lambda i: (0, 0, 0))
    edge = pl.BlockSpec((2, members + PAD, members), lambda i: (i, 0, 0))
    return pl.pallas_call(
        kernel,
        grid=(blocks // group,),
        in_specs=[
            pl.BlockSpec((members, group, cells), lambda i: (0, i, 0)),
            whole,
            whole,
            whole,
            pl.BlockSpec(memory_space=pltpu.SMEM),
        ],
        out_specs=[
            pl.BlockSpec((group, members, cells), lambda i: (i, 0, 0)),
            pl.BlockSpec((group, members + PAD, members), lambda i: (i, 0, 0)),
            edge,
            edge,
        ],
        out_shape=[
            jax.ShapeDtypeStruct((blocks, members, cells), BF16),
            jax.ShapeDtypeStruct((blocks, members + PAD, members), BF16),
            jax.ShapeDtypeStruct((lat, members + PAD, members), BF16),
            jax.ShapeDtypeStruct((lat, members + PAD, members), BF16),
        ],
        scratch_shapes=[
            pltpu.VMEM((cells // LANES, members * pitch, LANES), F32),
            pltpu.VMEM((2 * cols, members, slots), F32),
            pltpu.VMEM((2 * cols, members + PAD, slots), BF16),
        ],
        compiler_params=pltpu.CompilerParams(vmem_limit_bytes=VMEM_LIMIT),
        cost_estimate=cost(blocks, 0.27),
        name="select",
    )(state, cell, value, rinv, live)


def cost(blocks, micros):
    return pl.CostEstimate(
        flops=int(blocks * micros * 1.1e9), bytes_accessed=blocks * 1000, transcendentals=0
    )


def interleave(main, other):
    done = 0
    for i, unit in enumerate(main):
        unit()
        while done < len(other) and done * len(main) < (i + 1) * len(other):
            other[done]()
            done += 1
    for unit in other[done:]:
        unit()


def combine_units(sites, base, gh, pattern, cols, members, pq_f, pq_b, bd, norms, gains):
    ident = (
        lax.broadcasted_iota(jnp.int32, (members, members), 0)
        == lax.broadcasted_iota(jnp.int32, (members, members), 1)
    ).astype(F32)

    def unit(j, r, c):
        acc = None
        for n in range(9):
            term = gh[r - base[0] + n // 3, c - base[1] + n % 3].astype(F32)
            term = term * (TAPER_WEIGHTS[n] * pattern[r, c : c + 1, n : n + 1].astype(F32))
            acc = term if acc is None else acc + term
        info = acc[:members] + (members - 1) / INFLATION * ident
        gains[r, c] = acc[members : members + 1] + acc[members + 1 : members + 2]
        inv = lax.rsqrt(jnp.sum(jnp.sum(info * info, axis=0, keepdims=True), axis=1, keepdims=True))
        norms[r, c] = inv
        p = info * inv
        third = p * (1.0 / 3.0)
        q = ident - third
        pq_f[j, :members] = p
        pq_b[j, :members] = p.astype(BF16)
        pq_f[j, members:] = q
        pq_b[j, members:] = q.astype(BF16)
        bd[j] = third.astype(BF16)

    return [lambda j=j, r=r, c=c: unit(j, r, c) for j, (r, c) in enumerate(sites)]


def newton_units(count, members, pq_f, pq_b, bd):
    c = members

    def opening(j):
        p = pq_f[j, :c] - jnp.dot(pq_b[j, :c], bd[j], preferred_element_type=F32)
        pq_f[j, :c] = p
        pq_b[j, :c] = p.astype(BF16)

    def product(j, step):
        scale = 1.5 ** (2 * step) / 3.0
        prod = jnp.dot(pq_b[j, c:], pq_b[j, :c], preferred_element_type=F32)
        bd[j] = (prod * scale).astype(BF16)

    def update(j, step):
        start = 0 if step < NS_STEPS - 1 else c
        new = pq_f[j, start:] - jnp.dot(pq_b[j, start:], bd[j], preferred_element_type=F32)
        pq_f[j, start:] = new
        if start == 0:
            pq_b[j] = new.astype(BF16)

    units = [lambda j=j: opening(j) for j in range(count)]
    for step in range(1, NS_STEPS):
        for part in (product, update):
            units += [lambda j=j, step=step, part=part: part(j, step) for j in range(count)]
    return units


def transform_of(j, site, members, pq_f, norms, gains):
    q = pq_f[j, members:] * 1.5**NS_STEPS
    inv = norms[site]
    column = jnp.sum(q * gains[site], axis=1, keepdims=True)
    weights_row = jnp.sum(q * column, axis=0, keepdims=True) * inv
    return (q * jnp.sqrt((members - 1.0) * inv) + weights_row).astype(BF16)


def inner_transforms(gh, pattern, sites, first, depth, members, cols):
    c = members
    most = max(map(len, sites))
    total = sum(map(len, sites))

    def kernel(pattern_ref, gh_ref, out_ref, held, pq_f, pq_b, bd, sem):
        def fetch(i):
            return pltpu.make_async_copy(gh_ref.at[first + i], held.at[i], sem.at[i])

        for i in range(depth):
            fetch(i).start()
        norms, gains = {}, {}

        def combine(g):
            two = g % 2
            return combine_units(
                sites[g], (first + 1, 1), held, pattern_ref, cols, members,
                pq_f.at[two], pq_b.at[two], bd.at[two], norms, gains,
            )

        def finish(g):
            at = sum(map(len, sites[:g]))

            def unit(j, site):
                out_ref[at + j] = transform_of(j, site, members, pq_f.at[g % 2], norms, gains)

            return [lambda j=j, site=site: unit(j, site) for j, site in enumerate(sites[g])]

        for i in range(depth - len(sites) + 1):
            fetch(i).wait()
        interleave(combine(0), [])
        for g in range(len(sites)):
            beside = finish(g - 1) if g else []
            if g + 1 < len(sites):
                fetch(depth - len(sites) + 1 + g).wait()
                beside = beside + combine(g + 1)
            two = g % 2
            units = newton_units(len(sites[g]), members, pq_f.at[two], pq_b.at[two], bd.at[two])
            interleave(units, beside)
        interleave(finish(len(sites) - 1), [])

    return pl.pallas_call(
        kernel,
        in_specs=[pl.BlockSpec(memory_space=pltpu.VMEM), pl.BlockSpec(memory_space=pl.ANY)],
        out_specs=pl.BlockSpec(memory_space=pltpu.VMEM),
        out_shape=jax.ShapeDtypeStruct((total, members, members), BF16),
        scratch_shapes=[
            pltpu.VMEM((depth, cols, members + PAD, members), BF16),
            pltpu.VMEM((2, most, 2 * c, c), F32),
            pltpu.VMEM((2, most, 2 * c, c), BF16),
            pltpu.VMEM((2, most, c, c), BF16),
            pltpu.SemaphoreType.DMA((depth,)),
        ],
        compiler_params=pltpu.CompilerParams(vmem_limit_bytes=VMEM_LIMIT),
        cost_estimate=cost(total, 0.4),
        name="inner_transforms",
    )(pattern, gh)


def analyse(pattern, gh, west, east, beyond, xt, pairs, groups, ready, ready_sites):
    lat, cols, tall, members = gh.shape
    cells = xt.shape[2]
    c = members
    pitch = 2 * cols + 1
    most = max(map(len, groups))
    span = 2 * cols
    last_of = {p: max(g for g, sites in enumerate(groups) for r, _ in sites if r // 2 == p)
               for p in pairs}
    slot = {p: i for i, p in enumerate(pairs)}
    needed = [sorted({r + a for r, _ in sites for a in range(3)}) for sites in groups]
    fresh = [[r for r in rows if all(r not in old for old in needed[:g])]
             for g, rows in enumerate(needed)]
    sources = [pattern, gh, west, east, xt, *beyond, *ready]
    starts = [sum(map(len, ready_sites[:i])) for i in range(len(ready_sites))]

    def kernel(*refs):
        pattern_ref, gh_ref, west_ref, east_ref, xt_ref = refs[:5]
        beyond_refs = refs[5 : 5 + len(beyond)]
        ready_refs = refs[5 + len(beyond) : len(sources)]
        (out_ref, held, states, kept, pq_f, pq_b, bd, wide, narrow,
         row_sem, state_sem, kept_sem, out_sem) = refs[len(sources) :]

        def copy(src, dst, sem):
            pltpu.make_async_copy(src, dst, sem).start()

        for g, rows in enumerate(fresh):
            for r in rows:
                if r in (0, lat + 1):
                    copy(beyond_refs[r // (lat + 1)], held.at[r], row_sem.at[r])
                    continue
                copy(gh_ref.at[r - 1], held.at[r, pl.ds(1, cols)], row_sem.at[r])
                copy(west_ref.at[pl.ds(r - 1, 1)], held.at[r, pl.ds(0, 1)], row_sem.at[r])
                copy(east_ref.at[pl.ds(r - 1, 1)], held.at[r, pl.ds(cols + 1, 1)], row_sem.at[r])
            if g == 0:
                for i, ref in enumerate(ready_refs):
                    copy(ref, kept.at[pl.ds(starts[i], ref.shape[0])], kept_sem.at[i])
                for p in pairs:
                    copy(xt_ref.at[pl.ds(p * span, span)], states.at[slot[p]],
                         state_sem.at[slot[p]])

        def rows_in(g):
            for r in fresh[g]:
                pltpu.make_async_copy(held.at[r], held.at[r], row_sem.at[r]).wait()

        norms, gains = {}, {}

        def combine(g):
            two = g % 2
            return combine_units(
                groups[g], (0, 0), held, pattern_ref, cols, members,
                pq_f.at[two], pq_b.at[two], bd.at[two], norms, gains,
            )

        def apply(r, k, transform):
            ones = jnp.full((PAD, members), 1.0 / members, BF16)
            rest = 1.0 - jnp.sum(transform.astype(F32), axis=1, keepdims=True)
            left = jnp.concatenate([transform, ones], axis=0)
            at = r % 2 * cols + k
            out = jnp.dot(left, states[slot[r // 2], at], preferred_element_type=F32)
            out = out[:members] + rest * out[members : members + 1]
            for h in range(cells // LANES):
                wide[slot[r // 2], h, pl.ds(at, members, stride=pitch), :] = (
                    out[:, h * LANES : (h + 1) * LANES]
                )

        def finish(g):
            units = [
                lambda j=j, s=s: apply(
                    *s, transform_of(j, s, members, pq_f.at[g % 2], norms, gains)
                )
                for j, s in enumerate(groups[g])
            ]
            for p in pairs:
                if last_of[p] == g:
                    units += convert(slot[p])
            return units

        def sent(i):
            return pltpu.make_async_copy(
                narrow.at[i], out_ref.at[:, pl.ds(i * span, span)], out_sem.at[i]
            )

        def convert(i):
            def unit(start):
                for k in range(start, start + members // 8):
                    for h in range(cells // LANES):
                        part = wide[i, h, k * pitch : k * pitch + span, :]
                        narrow[i, k, :, h * LANES : (h + 1) * LANES] = part.astype(BF16)

            units = [lambda k=k: unit(k) for k in range(0, members, members // 8)]
            return units + [lambda: sent(i).start()]

        rows_in(0)
        interleave(combine(0), [])
        for i, ref in enumerate(ready_refs):
            part = kept.at[pl.ds(starts[i], ref.shape[0])]
            pltpu.make_async_copy(part, part, kept_sem.at[i]).wait()
        for p in pairs:
            i = slot[p]
            pltpu.make_async_copy(states.at[i], states.at[i], state_sem.at[i]).wait()
        for g in range(len(groups)):
            beside = [
                lambda i=i, s=s: apply(*s, kept[i])
                for i, s in enumerate(ready_sites[g], starts[g])
            ]
            beside = beside + (finish(g - 1) if g else [])
            if g + 1 < len(groups):
                rows_in(g + 1)
                beside = beside + combine(g + 1)
            two = g % 2
            units = newton_units(len(groups[g]), members, pq_f.at[two], pq_b.at[two], bd.at[two])
            interleave(units, beside)
        interleave(finish(len(groups) - 1), [])
        for p in pairs:
            sent(slot[p]).wait()

    any_spec = pl.BlockSpec(memory_space=pl.ANY)
    count = len(pairs)
    return pl.pallas_call(
        kernel,
        in_specs=[pl.BlockSpec(memory_space=pltpu.VMEM)] + [any_spec] * (len(sources) - 1),
        out_specs=any_spec,
        out_shape=jax.ShapeDtypeStruct((members, count * span, cells), BF16),
        scratch_shapes=[
            pltpu.VMEM((lat + 2, cols + 2, tall, members), BF16),
            pltpu.VMEM((count, span, members, cells), BF16),
            pltpu.VMEM((sum(map(len, ready_sites)), members, members), BF16),
            pltpu.VMEM((2, most, 2 * c, c), F32),
            pltpu.VMEM((2, most, 2 * c, c), BF16),
            pltpu.VMEM((2, most, c, c), BF16),
            pltpu.VMEM((count, cells // LANES, members * pitch, LANES), F32),
            pltpu.VMEM((count, members, span, cells), BF16),
            pltpu.SemaphoreType.DMA((lat + 2,)),
            pltpu.SemaphoreType.DMA((count,)),
            pltpu.SemaphoreType.DMA((len(ready),)),
            pltpu.SemaphoreType.DMA((count,)),
        ],
        compiler_params=pltpu.CompilerParams(vmem_limit_bytes=VMEM_LIMIT),
        cost_estimate=cost(count * span, 0.35),
        name="analyse",
    )(*sources)


def shift(value, axis, step, wrap):
    count = lax.axis_size(axis)
    pairs = [(i, (i + step) % count) for i in range(count) if wrap or 0 <= i + step < count]
    return lax.ppermute(value, axis, pairs)


def shards(members, obs_cell, obs_value, obs_rinv, obs_count, loc_pattern):
    mem_count = lax.axis_size("mem")
    blk_count = lax.axis_size("blk")
    devices = mem_count * blk_count
    lat_all, lon_all, cells = members.shape[1:]
    lat, lon = lat_all // mem_count, lon_all // blk_count
    slots = obs_cell.shape[2]

    tiled = members.reshape(mem_count, lat, blk_count, lon, cells).transpose(0, 2, 1, 3, 4)
    arrived = lax.all_to_all(
        tiled.reshape(devices, lat * lon, cells), AXES, split_axis=0, concat_axis=0, tiled=True
    )
    xt, gh, first, last = select(arrived, obs_cell, obs_value, obs_rinv, obs_count)
    gh = gh.reshape(lat, lon, *gh.shape[1:])
    west = shift(last, "blk", 1, True)
    east = shift(first, "blk", -1, True)
    half = lat // 2
    inner = [
        [(r, c) for r in rows for c in range(1, lon - 1)]
        for rows in (range(1, half), range(half, lat - 1))
    ]
    ready = [
        inner_transforms(gh, loc_pattern, [sites], start, half + 1, devices, lon)
        for sites, start in zip(inner, (0, half - 1))
    ]
    rim = [
        [(r, c) for r in rows for c in range(lon) if (r, c) not in inner[0] + inner[1]]
        for rows in ((0, 1, lat - 2, lat - 1), range(2, lat - 2))
    ]

    def full_row(r):
        return jnp.concatenate([west[r][None], gh[r], east[r][None]], axis=0)

    south = shift(full_row(lat - 1), "mem", 1, False)
    north = shift(full_row(0), "mem", -1, False)
    result = analyse(
        loc_pattern, gh, west, east, [south, north], xt, tuple(range(half)), rim, ready, inner
    )
    back = lax.all_to_all(result, AXES, split_axis=0, concat_axis=0, tiled=True)
    back = back.reshape(mem_count, blk_count, lat, lon, cells).transpose(0, 2, 1, 3, 4)
    return back.reshape(1, lat_all, lon_all, cells)


def solution(mesh):
    in_specs = (
        P(AXES, None, None, None),
        P("mem", "blk", None),
        P("mem", "blk", None),
        P("mem", "blk", None),
        P("mem", "blk"),
        P("mem", "blk", None),
    )
    out_specs = P(AXES, None, None, None)
    return jax.shard_map(shards, mesh=mesh, in_specs=in_specs, out_specs=out_specs, check_vma=False)
```

```python
import jax
import jax.numpy as jnp
from jax import lax
from jax.experimental import pallas as pl
from jax.experimental.pallas import tpu as pltpu
from jax.sharding import PartitionSpec as P

NS_STEPS = 5
TAPER_WEIGHTS = (0.3, 0.6, 0.3, 0.6, 1.0, 0.6, 0.3, 0.6, 0.3)
INFLATION = 1.1
F32 = jnp.float32
BF16 = jnp.bfloat16
PAD = 16
LANES = 128
AXES = ("mem", "blk")
VMEM_LIMIT = 62 * 1024 * 1024


def select(state, cell, value, rinv, live):
    members, _, cells = state.shape
    lat, cols, slots = cell.shape
    blocks = lat * cols
    group = 2 * cols
    pitch = group + 1

    def kernel(x_ref, cell_ref, value_ref, rinv_ref, live_ref, xt_ref, gh_ref, first_ref, last_ref, wide, seen, left_ref):
        for k in range(members):
            part = x_ref[k].astype(F32)
            for h in range(cells // LANES):
                wide[h, k * pitch : k * pitch + group, :] = part[:, h * LANES : (h + 1) * LANES]
        ids = lax.broadcasted_iota(jnp.int32, (cells, slots), 0)
        pad_row = lax.broadcasted_iota(jnp.int32, (PAD, slots), 0)
        slot = lax.broadcasted_iota(jnp.int32, (1, slots), 1)
        step = pl.program_id(0)

        means = []
        for b in range(2 * cols):
            half, j = divmod(b, cols)
            row = 2 * step + half
            own = jnp.concatenate(
                [
                    wide[h, pl.ds(b, members, stride=pitch), :].astype(BF16)
                    for h in range(cells // LANES)
                ],
                axis=1,
            )
            xt_ref[b] = own
            selector = (ids == cell_ref[row, j : j + 1, :]).astype(BF16)
            obs = jnp.dot(own, selector, preferred_element_type=F32)
            seen[b] = obs
            means.append(jnp.sum(obs, axis=0, keepdims=True) * (1.0 / members))
        for b in range(2 * cols):
            half, j = divmod(b, cols)
            row = 2 * step + half
            weight = jnp.where(slot < live_ref[row, j], rinv_ref[row, j : j + 1, :], 0.0)
            scale = jnp.sqrt(weight)
            depart = (value_ref[row, j : j + 1, :] - means[b]) * scale
            high = depart.astype(BF16).astype(F32)
            extra = jnp.where(pad_row == 0, high, jnp.where(pad_row == 1, depart - high, 0.0))
            left_ref[b, :members] = ((seen[b] - means[b]) * scale).astype(BF16)
            left_ref[b, members:] = extra.astype(BF16)
        for b in range(2 * cols):
            half, j = divmod(b, cols)
            gram = lax.dot_general(
                left_ref[b],
                left_ref[b, :members],
                (((1,), (1,)), ((), ())),
                preferred_element_type=F32,
            )
            gain = gram[members : members + 1] + gram[members + 1 : members + 2]
            upper = gain.astype(BF16).astype(F32)
            tail = jnp.where(pad_row == 0, upper, jnp.where(pad_row == 1, gain - upper, 0.0))
            gram = gram[:members].astype(BF16)
            tail = tail.astype(BF16)
            targets = [gh_ref.at[b]]
            targets += [first_ref.at[half]] if j == 0 else []
            targets += [last_ref.at[half]] if j == cols - 1 else []
            for target in targets:
                target[:members] = gram
                target[members:] = tail

    whole = pl.BlockSpec(cell.shape, lambda i: (0, 0, 0))
    edge = pl.BlockSpec((2, members + PAD, members), lambda i: (i, 0, 0))
    return pl.pallas_call(
        kernel,
        grid=(blocks // group,),
        in_specs=[
            pl.BlockSpec((members, group, cells), lambda i: (0, i, 0)),
            whole,
            whole,
            whole,
            pl.BlockSpec(memory_space=pltpu.SMEM),
        ],
        out_specs=[
            pl.BlockSpec((group, members, cells), lambda i: (i, 0, 0)),
            pl.BlockSpec((group, members + PAD, members), lambda i: (i, 0, 0)),
            edge,
            edge,
        ],
        out_shape=[
            jax.ShapeDtypeStruct((blocks, members, cells), BF16),
            jax.ShapeDtypeStruct((blocks, members + PAD, members), BF16),
            jax.ShapeDtypeStruct((lat, members + PAD, members), BF16),
            jax.ShapeDtypeStruct((lat, members + PAD, members), BF16),
        ],
        scratch_shapes=[
            pltpu.VMEM((cells // LANES, members * pitch, LANES), F32),
            pltpu.VMEM((2 * cols, members, slots), F32),
            pltpu.VMEM((2 * cols, members + PAD, slots), BF16),
        ],
        compiler_params=pltpu.CompilerParams(vmem_limit_bytes=VMEM_LIMIT),
        cost_estimate=cost(blocks, 0.27),
        name="select",
    )(state, cell, value, rinv, live)


def cost(blocks, micros):
    return pl.CostEstimate(
        flops=int(blocks * micros * 1.1e9), bytes_accessed=blocks * 1000, transcendentals=0
    )


def interleave(main, other):
    done = 0
    for i, unit in enumerate(main):
        unit()
        while done < len(other) and done * len(main) < (i + 1) * len(other):
            other[done]()
            done += 1
    for unit in other[done:]:
        unit()


def combine_units(sites, base, gh, pattern, cols, members, pq_f, pq_b, bd, norms, gains):
    ident = (
        lax.broadcasted_iota(jnp.int32, (members, members), 0)
        == lax.broadcasted_iota(jnp.int32, (members, members), 1)
    ).astype(F32)

    def unit(j, r, c):
        acc = None
        for n in range(9):
            term = gh[r - base[0] + n // 3, c - base[1] + n % 3].astype(F32)
            term = term * (TAPER_WEIGHTS[n] * pattern[r, c : c + 1, n : n + 1].astype(F32))
            acc = term if acc is None else acc + term
        info = acc[:members] + (members - 1) / INFLATION * ident
        gains[r, c] = acc[members : members + 1] + acc[members + 1 : members + 2]
        inv = lax.rsqrt(jnp.sum(jnp.sum(info * info, axis=0, keepdims=True), axis=1, keepdims=True))
        norms[r, c] = inv
        p = info * inv
        third = p * (1.0 / 3.0)
        q = ident - third
        pq_f[j, :members] = p
        pq_b[j, :members] = p.astype(BF16)
        pq_f[j, members:] = q
        pq_b[j, members:] = q.astype(BF16)
        bd[j] = third.astype(BF16)

    return [lambda j=j, r=r, c=c: unit(j, r, c) for j, (r, c) in enumerate(sites)]


def newton_units(count, members, pq_f, pq_b, bd):
    c = members

    def opening(j):
        p = pq_f[j, :c] - jnp.dot(pq_b[j, :c], bd[j], preferred_element_type=F32)
        pq_f[j, :c] = p
        pq_b[j, :c] = p.astype(BF16)

    def product(j, step):
        scale = 1.5 ** (2 * step) / 3.0
        prod = jnp.dot(pq_b[j, c:], pq_b[j, :c], preferred_element_type=F32)
        bd[j] = (prod * scale).astype(BF16)

    def update(j, step):
        start = 0 if step < NS_STEPS - 1 else c
        new = pq_f[j, start:] - jnp.dot(pq_b[j, start:], bd[j], preferred_element_type=F32)
        pq_f[j, start:] = new
        if start == 0:
            pq_b[j] = new.astype(BF16)

    units = [lambda j=j: opening(j) for j in range(count)]
    for step in range(1, NS_STEPS):
        for part in (product, update):
            units += [lambda j=j, step=step, part=part: part(j, step) for j in range(count)]
    return units


def transform_of(j, site, members, pq_f, norms, gains):
    q = pq_f[j, members:] * 1.5**NS_STEPS
    inv = norms[site]
    column = jnp.sum(q * gains[site], axis=1, keepdims=True)
    weights_row = jnp.sum(q * column, axis=0, keepdims=True) * inv
    return (q * jnp.sqrt((members - 1.0) * inv) + weights_row).astype(BF16)


def inner_transforms(gh, pattern, sites, first, depth, members, cols):
    c = members
    most = max(map(len, sites))
    total = sum(map(len, sites))

    def kernel(pattern_ref, gh_ref, out_ref, held, pq_f, pq_b, bd, sem):
        def fetch(i):
            return pltpu.make_async_copy(gh_ref.at[first + i], held.at[i], sem.at[i])

        for i in range(depth):
            fetch(i).start()
        norms, gains = {}, {}

        def combine(g):
            two = g % 2
            return combine_units(
                sites[g], (first + 1, 1), held, pattern_ref, cols, members,
                pq_f.at[two], pq_b.at[two], bd.at[two], norms, gains,
            )

        def finish(g):
            at = sum(map(len, sites[:g]))

            def unit(j, site):
                out_ref[at + j] = transform_of(j, site, members, pq_f.at[g % 2], norms, gains)

            return [lambda j=j, site=site: unit(j, site) for j, site in enumerate(sites[g])]

        for i in range(depth - len(sites) + 1):
            fetch(i).wait()
        interleave(combine(0), [])
        for g in range(len(sites)):
            beside = finish(g - 1) if g else []
            if g + 1 < len(sites):
                fetch(depth - len(sites) + 1 + g).wait()
                beside = beside + combine(g + 1)
            two = g % 2
            units = newton_units(len(sites[g]), members, pq_f.at[two], pq_b.at[two], bd.at[two])
            interleave(units, beside)
        interleave(finish(len(sites) - 1), [])

    return pl.pallas_call(
        kernel,
        in_specs=[pl.BlockSpec(memory_space=pltpu.VMEM), pl.BlockSpec(memory_space=pl.ANY)],
        out_specs=pl.BlockSpec(memory_space=pltpu.VMEM),
        out_shape=jax.ShapeDtypeStruct((total, members, members), BF16),
        scratch_shapes=[
            pltpu.VMEM((depth, cols, members + PAD, members), BF16),
            pltpu.VMEM((2, most, 2 * c, c), F32),
            pltpu.VMEM((2, most, 2 * c, c), BF16),
            pltpu.VMEM((2, most, c, c), BF16),
            pltpu.SemaphoreType.DMA((depth,)),
        ],
        compiler_params=pltpu.CompilerParams(vmem_limit_bytes=VMEM_LIMIT),
        cost_estimate=cost(total, 0.4),
        name="inner_transforms",
    )(pattern, gh)


def analyse(pattern, gh, west, east, beyond, xt, pairs, groups, ready, ready_sites):
    lat, cols, tall, members = gh.shape
    cells = xt.shape[2]
    c = members
    pitch = 2 * cols + 1
    most = max(map(len, groups))
    span = 2 * cols
    last_of = {p: max(g for g, sites in enumerate(groups) for r, _ in sites if r // 2 == p)
               for p in pairs}
    slot = {p: i for i, p in enumerate(pairs)}
    needed = [sorted({r + a for r, _ in sites for a in range(3)}) for sites in groups]
    fresh = [[r for r in rows if all(r not in old for old in needed[:g])]
             for g, rows in enumerate(needed)]
    sources = [pattern, gh, west, east, xt, *beyond, *ready]
    starts = [sum(map(len, ready_sites[:i])) for i in range(len(ready_sites))]

    def kernel(*refs):
        pattern_ref, gh_ref, west_ref, east_ref, xt_ref = refs[:5]
        beyond_refs = refs[5 : 5 + len(beyond)]
        ready_refs = refs[5 + len(beyond) : len(sources)]
        (out_ref, held, states, kept, pq_f, pq_b, bd, wide, narrow,
         row_sem, state_sem, kept_sem, out_sem) = refs[len(sources) :]

        def copy(src, dst, sem):
            pltpu.make_async_copy(src, dst, sem).start()

        for g, rows in enumerate(fresh):
            for r in rows:
                if r in (0, lat + 1):
                    copy(beyond_refs[r // (lat + 1)], held.at[r], row_sem.at[r])
                    continue
                copy(gh_ref.at[r - 1], held.at[r, pl.ds(1, cols)], row_sem.at[r])
                copy(west_ref.at[pl.ds(r - 1, 1)], held.at[r, pl.ds(0, 1)], row_sem.at[r])
                copy(east_ref.at[pl.ds(r - 1, 1)], held.at[r, pl.ds(cols + 1, 1)], row_sem.at[r])
            if g == 0:
                for i, ref in enumerate(ready_refs):
                    copy(ref, kept.at[pl.ds(starts[i], ref.shape[0])], kept_sem.at[i])
                for p in pairs:
                    copy(xt_ref.at[pl.ds(p * span, span)], states.at[slot[p]],
                         state_sem.at[slot[p]])

        def rows_in(g):
            for r in fresh[g]:
                pltpu.make_async_copy(held.at[r], held.at[r], row_sem.at[r]).wait()

        norms, gains = {}, {}

        def combine(g):
            two = g % 2
            return combine_units(
                groups[g], (0, 0), held, pattern_ref, cols, members,
                pq_f.at[two], pq_b.at[two], bd.at[two], norms, gains,
            )

        def apply(r, k, transform):
            ones = jnp.full((PAD, members), 1.0 / members, BF16)
            rest = 1.0 - jnp.sum(transform.astype(F32), axis=1, keepdims=True)
            left = jnp.concatenate([transform, ones], axis=0)
            at = r % 2 * cols + k
            out = jnp.dot(left, states[slot[r // 2], at], preferred_element_type=F32)
            out = out[:members] + rest * out[members : members + 1]
            for h in range(cells // LANES):
                wide[slot[r // 2], h, pl.ds(at, members, stride=pitch), :] = (
                    out[:, h * LANES : (h + 1) * LANES]
                )

        def finish(g):
            units = [
                lambda j=j, s=s: apply(
                    *s, transform_of(j, s, members, pq_f.at[g % 2], norms, gains)
                )
                for j, s in enumerate(groups[g])
            ]
            for p in pairs:
                if last_of[p] == g:
                    units += convert(slot[p])
            return units

        def sent(i):
            return pltpu.make_async_copy(
                narrow.at[i], out_ref.at[:, pl.ds(i * span, span)], out_sem.at[i]
            )

        def convert(i):
            def unit(start):
                for k in range(start, start + members // 8):
                    for h in range(cells // LANES):
                        part = wide[i, h, k * pitch : k * pitch + span, :]
                        narrow[i, k, :, h * LANES : (h + 1) * LANES] = part.astype(BF16)

            units = [lambda k=k: unit(k) for k in range(0, members, members // 8)]
            return units + [lambda: sent(i).start()]

        rows_in(0)
        interleave(combine(0), [])
        for i, ref in enumerate(ready_refs):
            part = kept.at[pl.ds(starts[i], ref.shape[0])]
            pltpu.make_async_copy(part, part, kept_sem.at[i]).wait()
        for p in pairs:
            i = slot[p]
            pltpu.make_async_copy(states.at[i], states.at[i], state_sem.at[i]).wait()
        for g in range(len(groups)):
            beside = [
                lambda i=i, s=s: apply(*s, kept[i])
                for i, s in enumerate(ready_sites[g], starts[g])
            ]
            beside = beside + (finish(g - 1) if g else [])
            if g + 1 < len(groups):
                rows_in(g + 1)
                beside = beside + combine(g + 1)
            two = g % 2
            units = newton_units(len(groups[g]), members, pq_f.at[two], pq_b.at[two], bd.at[two])
            interleave(units, beside)
        interleave(finish(len(groups) - 1), [])
        for p in pairs:
            sent(slot[p]).wait()

    any_spec = pl.BlockSpec(memory_space=pl.ANY)
    count = len(pairs)
    return pl.pallas_call(
        kernel,
        in_specs=[pl.BlockSpec(memory_space=pltpu.VMEM)] + [any_spec] * (len(sources) - 1),
        out_specs=any_spec,
        out_shape=jax.ShapeDtypeStruct((members, count * span, cells), BF16),
        scratch_shapes=[
            pltpu.VMEM((lat + 2, cols + 2, tall, members), BF16),
            pltpu.VMEM((count, span, members, cells), BF16),
            pltpu.VMEM((sum(map(len, ready_sites)), members, members), BF16),
            pltpu.VMEM((2, most, 2 * c, c), F32),
            pltpu.VMEM((2, most, 2 * c, c), BF16),
            pltpu.VMEM((2, most, c, c), BF16),
            pltpu.VMEM((count, cells // LANES, members * pitch, LANES), F32),
            pltpu.VMEM((count, members, span, cells), BF16),
            pltpu.SemaphoreType.DMA((lat + 2,)),
            pltpu.SemaphoreType.DMA((count,)),
            pltpu.SemaphoreType.DMA((len(ready),)),
            pltpu.SemaphoreType.DMA((count,)),
        ],
        compiler_params=pltpu.CompilerParams(vmem_limit_bytes=VMEM_LIMIT),
        cost_estimate=cost(count * span, 0.35),
        name="analyse",
    )(*sources)


def shift(value, axis, step, wrap):
    count = lax.axis_size(axis)
    pairs = [(i, (i + step) % count) for i in range(count) if wrap or 0 <= i + step < count]
    return lax.ppermute(value, axis, pairs)


def shards(members, obs_cell, obs_value, obs_rinv, obs_count, loc_pattern):
    mem_count = lax.axis_size("mem")
    blk_count = lax.axis_size("blk")
    devices = mem_count * blk_count
    lat_all, lon_all, cells = members.shape[1:]
    lat, lon = lat_all // mem_count, lon_all // blk_count
    slots = obs_cell.shape[2]

    tiled = members.reshape(mem_count, lat, blk_count, lon, cells).transpose(0, 2, 1, 3, 4)
    arrived = lax.all_to_all(
        tiled.reshape(devices, lat * lon, cells), AXES, split_axis=0, concat_axis=0, tiled=True
    )
    xt, gh, first, last = select(arrived, obs_cell, obs_value, obs_rinv, obs_count)
    gh = gh.reshape(lat, lon, *gh.shape[1:])
    west = shift(last, "blk", 1, True)
    east = shift(first, "blk", -1, True)
    half = lat // 2
    inner = [
        [(r, c) for r in rows for c in range(1, lon - 1)]
        for rows in (range(1, half + 1), range(half + 1, lat - 1))
    ]
    ready = [
        inner_transforms(gh, loc_pattern, [sites], start, depth, devices, lon)
        for sites, start, depth in zip(inner, (0, half), (half + 2, lat - half))
    ]
    rim = [
        [(r, c) for r in rows for c in range(lon) if (r, c) not in inner[0] + inner[1]]
        for rows in ((0, 1, lat - 2, lat - 1), range(2, lat - 2))
    ]

    def full_row(r):
        return jnp.concatenate([west[r][None], gh[r], east[r][None]], axis=0)

    south = shift(full_row(lat - 1), "mem", 1, False)
    north = shift(full_row(0), "mem", -1, False)
    result = analyse(
        loc_pattern, gh, west, east, [south, north], xt, tuple(range(half)), rim, ready, inner
    )
    back = lax.all_to_all(result, AXES, split_axis=0, concat_axis=0, tiled=True)
    back = back.reshape(mem_count, blk_count, lat, lon, cells).transpose(0, 2, 1, 3, 4)
    return back.reshape(1, lat_all, lon_all, cells)


def solution(mesh):
    in_specs = (
        P(AXES, None, None, None),
        P("mem", "blk", None),
        P("mem", "blk", None),
        P("mem", "blk", None),
        P("mem", "blk"),
        P("mem", "blk", None),
    )
    out_specs = P(AXES, None, None, None)
    return jax.shard_map(shards, mesh=mesh, in_specs=in_specs, out_specs=out_specs, check_vma=False)
```
